512 devices in a mesh: section: 8 (over z_lo), seq: 64 (over z_hi, x, y, core).
Axes of the slice: x: 4, y: 4, z: 16 (z_hi: 2, z_lo: 8; z = z_hi * 8 + z_lo), core: 2. Of those that a mesh axis runs over, the one named last changes fastest.
Arguments:
- queries: bfloat16 [24576, 4096], P('seq', 'section'), may hold values from -8 to 8
- enc_keys: bfloat16 [512, 4096], P(('section', 'seq')), may hold values from -8 to 8
- enc_values: bfloat16 [512, 4096], P(('section', 'seq')), may hold values from -6 to 6
- out_grad: bfloat16 [24576, 4096], P('seq', 'section'), may hold values from -6 to 6
- enc_doc: int32 [512], replicated, may hold values from 0 to 3, never falling along the last dimension, each value on 1 to 256 neighbouring positions
- dec_doc: int32 [24576], P('seq'), may hold values from 0 to 3, never falling along the last dimension, each value on 1 to 12288 neighbouring positions
Outputs:
- context: bfloat16 [24576, 4096], P('seq', 'section')
- query_grad: float32 [24576, 4096], P('seq', 'section')
- key_grad: float32 [512, 4096], P(('section', 'seq'))
- value_grad: float32 [512, 4096], P(('section', 'seq'))
The draws below stay inside these ranges and needn't reach their ends.
Inputs may be any that keep to these rules, and one draw needn't show every extreme that they name: `enc_doc`: never falls along the positions; every document number occurs. `dec_doc`: never falls along the positions; every document number occurs.
All inputs are finite; a program needn't handle non-finite values.
Results may differ from the reference program's by a relative error of at most 0.02.
The reference program's roundings to bfloat16 on the way (of `weights` and `dscore`) count: a program that leaves them out, or rounds other values in their place, can miss the bound.
Values may be sent and summed in bfloat16 or wider, within the bound.
No kernel may reach another device: no remote copies, remote signals or barrier semaphores. Data moves between devices by JAX's collectives and lax.ppermute only.
A program may use at most 64 MiB of HBM per device.

```python
import math
import jax
import jax.numpy as jnp
import numpy as np
from jax import lax

HEADS = 16
HD = 256
DOCS = 4
LQ = 24576
LE = 512


def draw_queries(key, part):
    base_normal = jax.random.normal(jax.random.fold_in(key, 11), (LQ, HEADS * HD), jnp.float32)
    return jnp.clip(2.0 * base_normal, -8.0, 8.0).astype(jnp.bfloat16)


def draw_enc_keys(key, part):
    base_normal = jax.random.normal(jax.random.fold_in(key, 21), (LE, HEADS * HD), jnp.float32)
    return jnp.clip(base_normal, -6.0, 6.0).astype(jnp.bfloat16)


def block_scale(rng, shape, split, low, top_value):
    def one(axis_at, parts):
        heights = jax.random.uniform(jax.random.fold_in(jax.random.fold_in(rng, 6), axis_at), (parts,), jnp.float32, low / len(split), top_value / len(split))
        return jnp.repeat(jnp.exp(heights), shape[axis_at] // parts).reshape((-1,) + (1,) * (len(shape) - axis_at - 1))

    factor_of = one(*split[0])
    for cut in split[1:]:
        factor_of = factor_of * one(*cut)
    return factor_of


def length_profile(amount, total, reach, skew):
    loads = [(1 << 20) // math.isqrt(grade ** skew) + 1 for grade in range(2, amount + 1)]
    spare, given = total - reach - (amount - 1), [1] * (amount - 1)
    while spare > 0:
        movable = [i for i in range(amount - 1) if given[i] < reach]
        whole, left = sum([loads[i] for i in movable]), spare
        for i in movable:
            addition = min(reach - given[i], max(1, left * loads[i] // whole), spare)
            given[i] = given[i] + addition
            spare = spare - addition
    return np.array([reach] + given)


def ragged_sizes(stream_key, amount, total, limit, lean):
    if amount == 2:
        one = jax.random.randint(stream_key, (), max(1, total - limit), min(limit, total - 1) + 1)
        return jnp.stack([one, total - one])
    sizes = jnp.asarray(length_profile(amount, total, limit, lean), jnp.int32)
    twos = (amount - 1) // 2
    donor, sink = sizes[1:1 + 2 * twos:2], sizes[2:2 + 2 * twos:2]
    margin = jnp.minimum(donor - 1, limit - sink)
    moved = jax.random.randint(jax.random.fold_in(stream_key, 1), (twos,), 0, 1 << 20) % (margin + 1)
    sizes = sizes.at[1:1 + 2 * twos:2].set(donor - moved).at[2:2 + 2 * twos:2].set(sink + moved)
    return sizes[jax.random.permutation(jax.random.fold_in(stream_key, 2), amount)]


def centred(own_key, shape, scale, limit, split=(), held_as=jnp.bfloat16):
    result = scale * jax.random.normal(own_key, shape, jnp.float32)
    if split:
        result = result * block_scale(own_key, shape, split, -0.22, 0.18)
    return jnp.clip(result, -limit, limit).astype(held_as)


def setup_inputs(seed: int = 0) -> dict:
    keys = jax.random.split(jax.random.key(seed), 7)
    return {
        "queries": draw_queries(jax.random.fold_in(keys[6], 71), 0),
        "enc_keys": draw_enc_keys(jax.random.fold_in(keys[6], 71), 0),
        "enc_values": centred(keys[2], (LE, HEADS * HD), 1.0, 6.0, ((0, 512),)),
        "out_grad": centred(keys[3], (LQ, HEADS * HD), 1.0, 6.0, ((0, 64), (1, 8))),
        "enc_doc": jnp.searchsorted(jnp.cumsum(ragged_sizes(keys[4], DOCS, LE, LE // 2, 2)), jnp.arange(LE), side="right").astype(jnp.int32),
        "dec_doc": jnp.searchsorted(jnp.cumsum(ragged_sizes(keys[5], DOCS, LQ, LQ // 2, 2)), jnp.arange(LQ), side="right").astype(jnp.int32),
    }


NEGATIVE = -1.0e30


def single_head(head_items, enc_doc, dec_doc):
    query_h, key_h, value_h, grad_h = head_items
    score_scale = HD ** -0.5
    allowed = dec_doc[:, None] == enc_doc[None, :]
    logits = jnp.where(allowed, jnp.dot(query_h, key_h.T, preferred_element_type=jnp.float32) * score_scale, NEGATIVE)
    row_max = jnp.max(logits, axis=1, keepdims=True)
    row_sum = jnp.sum(jnp.where(allowed, jnp.exp(logits - row_max), 0.0), axis=1, keepdims=True)
    log_sum = row_max + jnp.log(row_sum)
    probability = jnp.where(allowed, jnp.exp(logits - log_sum), 0.0)
    weights = probability.astype(jnp.bfloat16)
    context = jnp.dot(weights, value_h, preferred_element_type=jnp.float32).astype(jnp.bfloat16)
    row_delta = jnp.sum(grad_h.astype(jnp.float32) * context.astype(jnp.float32), axis=1, keepdims=True)
    prob_grad = jnp.dot(grad_h, value_h.T, preferred_element_type=jnp.float32)
    dscore = (probability * (prob_grad - row_delta)).astype(jnp.bfloat16)
    query_grad = jnp.dot(dscore, key_h, preferred_element_type=jnp.float32) * score_scale
    key_grad = jnp.dot(dscore.T, query_h, preferred_element_type=jnp.float32) * score_scale
    value_grad = jnp.dot(weights.T, grad_h, preferred_element_type=jnp.float32)
    return context, query_grad, key_grad, value_grad


def heads_first(matrix):
    return matrix.reshape(matrix.shape[0], HEADS, HD).transpose(1, 0, 2)


def heads_back(stacked):
    return stacked.transpose(1, 0, 2).reshape(stacked.shape[1], HEADS * HD)


def reference(queries, enc_keys, enc_values, out_grad, enc_doc, dec_doc):
    results = lax.map(lambda head_items: single_head(head_items, enc_doc, dec_doc),
                      (heads_first(queries), heads_first(enc_keys), heads_first(enc_values), heads_first(out_grad)))
    return (heads_back(results[0]), heads_back(results[1]), heads_back(results[2]), heads_back(results[3]))
```

```python
import jax
import jax.numpy as jnp
from jax import lax
from jax.experimental import pallas as pl
from jax.experimental.pallas import tpu as pltpu
from jax.sharding import Mesh, PartitionSpec as P

HD = 256
NEGATIVE = -1e30
NT = (((1,), (1,)), ((), ()))
NN = (((1,), (0,)), ((), ()))
TN = (((0,), (0,)), ((), ()))


def dot(a, b, dims):
    return lax.dot_general(a, b, dims, preferred_element_type=jnp.float32)


def attention_kernel(
    q_ref, g_ref, own_ref, other_ref, ed_ref, dd_ref, ctx_ref, dq_ref, down_ref, dother_ref
):
    half, wide = own_ref.shape
    cols = wide // 2
    scale = HD**-0.5
    allowed = dd_ref[...] == ed_ref[...]
    for head in range(cols // HD):
        at = slice(head * HD, (head + 1) * HD)
        at_v = slice(cols + head * HD, cols + (head + 1) * HD)
        q, g = q_ref[:, at], g_ref[:, at]
        k = jnp.concatenate([own_ref[:, at], other_ref[:, at]], axis=0)
        v = jnp.concatenate([own_ref[:, at_v], other_ref[:, at_v]], axis=0)
        logits = jnp.where(allowed, dot(q, k, NT) * scale, NEGATIVE)
        top = jnp.max(logits, axis=1, keepdims=True)
        terms = jnp.exp(logits - top)
        prob = terms * (1.0 / jnp.sum(terms, axis=1, keepdims=True))
        weights = prob.astype(jnp.bfloat16)
        ctx = dot(weights, v, NN).astype(jnp.bfloat16)
        ctx_ref[:, at] = ctx
        delta = jnp.sum(
            g.astype(jnp.float32) * ctx.astype(jnp.float32), axis=1, keepdims=True
        )
        ds = (prob * (dot(g, v, NT) - delta)).astype(jnp.bfloat16)
        dq_ref[:, at] = dot(ds, k, NN) * scale
        dk = dot(ds, q, TN) * scale
        dv = dot(weights, g, TN)
        down_ref[:, at] = dk[:half]
        down_ref[:, at_v] = dv[:half]
        dother_ref[:, at] = dk[half:].astype(jnp.bfloat16)
        dother_ref[:, at_v] = dv[half:].astype(jnp.bfloat16)


def attention(q, g, own, other, ed, dd):
    rows, cols = q.shape
    return pl.pallas_call(
        attention_kernel,
        out_shape=[
            jax.ShapeDtypeStruct((rows, cols), jnp.bfloat16),
            jax.ShapeDtypeStruct((rows, cols), jnp.float32),
            jax.ShapeDtypeStruct(own.shape, jnp.float32),
            jax.ShapeDtypeStruct(own.shape, jnp.bfloat16),
        ],
        compiler_params=pltpu.CompilerParams(vmem_limit_bytes=48 * 1024 * 1024),
        cost_estimate=pl.CostEstimate(
            flops=24 * rows * own.size // 2,
            bytes_accessed=6 * 1024 * 1024,
            transcendentals=rows * own.shape[0] * 2 * cols // HD,
        ),
    )(q, g, own, other, ed, dd)


def body(queries, enc_keys, enc_values, out_grad, enc_doc, dec_doc):
    size = {a: lax.axis_size(a) for a in "shxyc"}
    rows, cols = queries.shape
    sections, column = size["s"] * size["h"], size["x"] * size["y"]
    pair = [(0, 1), (1, 0)]
    parts = jnp.concatenate(
        [enc_keys.reshape(size["s"], -1, 128), enc_values.reshape(size["s"], -1, 128)], axis=1
    )
    parts = jnp.broadcast_to(parts[None], (size["h"],) + parts.shape)
    parts = parts.reshape((sections,) + parts.shape[2:])
    mine = lax.all_to_all(parts, ("h", "s"), split_axis=0, concat_axis=0, tiled=True)
    mine = mine.reshape(sections, 2 * cols)
    spread = jnp.broadcast_to(mine[None], (column,) + mine.shape)
    own = lax.all_to_all(spread, ("x", "y"), split_axis=0, concat_axis=0, tiled=True)
    own = own.reshape(column * sections, 2 * cols)
    other = lax.ppermute(own, "c", pair)
    docs = enc_doc.reshape([size[a] for a in "shxyc"]).transpose(4, 2, 3, 1, 0)
    docs = docs.reshape(2, -1)
    docs = jnp.where(lax.axis_index("c") == 0, docs, docs[::-1]).reshape(1, -1)
    context, query_grad, grad_own, grad_other = attention(
        queries, out_grad, own, other, docs, dec_doc.reshape(-1, 1)
    )
    came = lax.ppermute(grad_other, "c", pair)
    chip = (grad_own + came.astype(jnp.float32)).astype(jnp.bfloat16)
    chip = chip.reshape(column, sections, 2 * cols)
    plane = lax.all_to_all(chip, ("x", "y"), split_axis=0, concat_axis=0, tiled=True)
    plane = jnp.sum(plane.astype(jnp.float32), axis=0).astype(jnp.bfloat16)
    plane = plane.reshape(sections, -1, 128)
    last = lax.all_to_all(plane, ("h", "s"), split_axis=0, concat_axis=0, tiled=True)
    last = last.reshape((size["h"], size["s"]) + last.shape[1:]).astype(jnp.float32)
    last = jnp.sum(last, axis=0)
    blocks = cols // 128
    key_grad = last[:, :blocks].reshape(1, -1)
    value_grad = last[:, blocks:].reshape(1, -1)
    return context, query_grad, key_grad, value_grad


def solution(mesh):
    inner = Mesh(mesh.devices.reshape(8, 2, 4, 4, 2), ("s", "h", "x", "y", "c"))
    seq = ("h", "x", "y", "c")
    wide, owner = P(seq, "s"), P(("s",) + seq, None)
    return jax.shard_map(
        body,
        mesh=inner,
        in_specs=(wide, owner, owner, wide, P(), P(seq)),
        out_specs=(wide, wide, owner, owner),
        check_vma=False,
    )
```
